32 devices in a mesh: ha: 16 (over z, y, core), wa: 2 (over x).
Axes of the slice: x: 2, y: 2, z: 4, core: 2. Of those that a mesh axis runs over, the one named last changes fastest.
Arguments:
- density: bfloat16 [4, 8, 128, 256], P(None, None, 'ha', 'wa'), may hold values from -16 to 16
- kernel_one: bfloat16 [32, 4, 3, 3, 3], replicated, may hold values from -0.625 to 0.625
- kernel_two: bfloat16 [64, 32, 3, 3, 3], replicated, may hold values from -0.21875 to 0.21875
- kernel_three: bfloat16 [128, 64, 3, 3, 3], replicated, may hold values from -0.15625 to 0.15625
- dense_one: bfloat16 [4096, 128], replicated, may hold values from -0.1875 to 0.1875
- bias_one: float32 [128], replicated, may hold values from -3 to 3
- dense_two: bfloat16 [128, 64], replicated, may hold values from -0.5 to 0.5
- bias_two: float32 [64], replicated, may hold values from -3 to 3
- dense_three: bfloat16 [64, 4], replicated, may hold values from -0.75 to 0.75
- bias_three: float32 [4], replicated, may hold values from -4 to 4
- target: float32 [4], replicated, may hold values from -4 to 4
Outputs:
- grad_input: bfloat16 [4, 8, 128, 256], P(None, None, 'ha', 'wa')
- update_one: float32 [32, 4, 3, 3, 3], replicated
- update_two: float32 [64, 32, 3, 3, 3], replicated
- update_three: float32 [128, 64, 3, 3, 3], replicated
The draws below stay inside these ranges and needn't reach their ends.
All inputs are finite; a program needn't handle non-finite values.
Results may differ from the reference program's by a relative error of at most 0.012.
Values may be sent and summed in bfloat16 or wider, within the bound.
A program may use at most 128 MiB of HBM per device.

```python
import math
import jax
import jax.numpy as jnp
from jax import lax

C0 = 4
C1 = 32
C2 = 64
C3 = 128
H1 = 128
H2 = 64
NOUT = 4
DEP = 8
HD = 8
WD = 128
LOSS_SCALE = 1048576
H = 128
W = 256
GH = 16
GW = 2
NF = 4096


def draw_density(key, part):
    scale_key = jax.random.fold_in(key, 11)
    noise_key = jax.random.fold_in(key, 23)
    log_scale = jax.random.uniform(scale_key, (GH, GW), jnp.float32, math.log(0.25), math.log(4.0))
    region_scale = jnp.exp(log_scale)
    cell_scale = jnp.repeat(jnp.repeat(region_scale, HD, axis=0), WD, axis=1)
    noise = jnp.clip(jax.random.normal(noise_key, (C0, DEP, H, W), jnp.float32), -4.0, 4.0)
    return (noise * cell_scale[None, None, :, :]).astype(jnp.bfloat16)


def normal_values(own_key, dims, scale, most, dtype=jnp.bfloat16):
    values = scale * jax.random.normal(own_key, dims, jnp.float32)
    return jnp.clip(values, min=-most, max=most).astype(dtype)


def setup_inputs(seed: int = 0) -> dict:
    streams_of = jax.random.split(jax.random.key(seed), 12)
    return {
        "density": draw_density(jax.random.fold_in(streams_of[11], 71), 0),
        "kernel_one": normal_values(streams_of[1], (C1, C0, 3, 3, 3), (27 * C0) ** -0.5, 0.625),
        "kernel_two": normal_values(streams_of[2], (C2, C1, 3, 3, 3), (27 * C1) ** -0.5, 0.21875),
        "kernel_three": normal_values(streams_of[3], (C3, C2, 3, 3, 3), (27 * C2) ** -0.5, 0.15625),
        "dense_one": normal_values(streams_of[4], (NF, H1), (NF // 4) ** -0.5, 0.1875),
        "bias_one": normal_values(streams_of[5], (H1,), 0.5, 3.0, jnp.float32),
        "dense_two": normal_values(streams_of[6], (H1, H2), H1 ** -0.5, 0.5),
        "bias_two": normal_values(streams_of[7], (H2,), 0.5, 3.0, jnp.float32),
        "dense_three": normal_values(streams_of[8], (H2, NOUT), H2 ** -0.5, 0.75),
        "bias_three": normal_values(streams_of[9], (NOUT,), 1.0, 4.0, jnp.float32),
        "target": normal_values(streams_of[10], (NOUT,), 1.0, 4.0, jnp.float32),
    }


conv_layout = ('NCDHW', 'OIDHW', 'NCDHW')

def conv_same(field, kernel):
    result = lax.conv_general_dilated(field.astype(jnp.float32)[None], kernel.astype(jnp.float32), (1, 1, 1), ((1, 1), (1, 1), (1, 1)), dimension_numbers=conv_layout, precision=lax.Precision.HIGHEST)
    return result[0]

def flipped(kernel):
    return jnp.transpose(kernel, (1, 0, 2, 3, 4))[:, :, ::-1, ::-1, ::-1]

def silu_slope(values):
    sigmoid = jax.nn.sigmoid(values)
    return sigmoid * (1.0 + values * (1.0 - sigmoid))

def pooled(values):
    channels, depth_cells, row_cells, column_cells = values.shape
    return values.reshape(channels, depth_cells // 2, 2, row_cells // 2, 2, column_cells // 2, 2).mean(axis=(2, 4, 6))

def spread_up(values):
    channels, depth_cells, row_cells, column_cells = values.shape
    grown = jnp.broadcast_to(values[:, :, None, :, None, :, None], (channels, depth_cells, 2, row_cells, 2, column_cells, 2))
    return grown.reshape(channels, 2 * depth_cells, 2 * row_cells, 2 * column_cells)

def weight_grad(field, gradient):
    outputs, depth_cells, row_cells, column_cells = gradient.shape
    padded = jnp.pad(field.astype(jnp.float32), ((0, 0), (1, 1), (1, 1), (1, 1)))
    grad_wide = gradient.astype(jnp.float32)
    terms = []
    for depth_at in range(3):
        for row_at in range(3):
            for column_at in range(3):
                shifted = padded[:, depth_at:depth_at + depth_cells, row_at:row_at + row_cells, column_at:column_at + column_cells]
                terms.append(jnp.einsum('odhw,idhw->oi', grad_wide, shifted, precision=lax.Precision.HIGHEST))
    stacked = jnp.stack(terms, 0)
    return jnp.transpose(stacked.reshape(3, 3, 3, outputs, -1), (3, 4, 0, 1, 2))

def unit_scale(gradient):
    return gradient / jnp.sqrt(jnp.mean(gradient * gradient) + 1e-06)

def reference(density, kernel_one, kernel_two, kernel_three, dense_one, bias_one, dense_two, bias_two, dense_three, bias_three, target):
    z_one = conv_same(density, kernel_one)
    pooled_one = pooled(jax.nn.silu(z_one)).astype(jnp.bfloat16)
    z_two = conv_same(pooled_one, kernel_two)
    pooled_two = pooled(jax.nn.silu(z_two)).astype(jnp.bfloat16)
    z_three = conv_same(pooled_two, kernel_three)
    channels, depth_three, rows_three, columns_three = z_three.shape
    region_rows = rows_three // GH
    region_columns = columns_three // GW
    act_three = jax.nn.silu(z_three).reshape(channels, depth_three, GH, region_rows, GW, region_columns)
    features = jnp.transpose(act_three.mean(axis=(1, 3, 5)), (1, 2, 0)).reshape(-1).astype(jnp.bfloat16)
    pre_one = jnp.dot(features, dense_one, preferred_element_type=jnp.float32) + bias_one
    hidden_one = jax.nn.silu(pre_one)
    pre_two = jnp.dot(hidden_one, dense_two.astype(jnp.float32), precision=lax.Precision.HIGHEST) + bias_two
    hidden_two = jax.nn.silu(pre_two)
    output = jnp.dot(hidden_two, dense_three.astype(jnp.float32), precision=lax.Precision.HIGHEST) + bias_three
    grad_output = LOSS_SCALE * (output - target)
    grad_two = jnp.dot(dense_three.astype(jnp.float32), grad_output, precision=lax.Precision.HIGHEST) * silu_slope(pre_two)
    grad_one = jnp.dot(dense_two.astype(jnp.float32), grad_two, precision=lax.Precision.HIGHEST) * silu_slope(pre_one)
    grad_features = jnp.dot(dense_one.astype(jnp.float32), grad_one, precision=lax.Precision.HIGHEST)
    per_region = jnp.transpose(grad_features.reshape(GH, GW, channels), (2, 0, 1))
    spread = jnp.broadcast_to(per_region[:, None, :, None, :, None], (channels, depth_three, GH, region_rows, GW, region_columns)).reshape(channels, depth_three, rows_three, columns_three)
    region_cells = depth_three * region_rows * region_columns
    grad_three = (spread / region_cells * silu_slope(z_three)).astype(jnp.bfloat16)
    weights_three = weight_grad(pooled_two, grad_three)
    back_two = conv_same(grad_three, flipped(kernel_three))
    grad_two_field = (spread_up(back_two) * 0.125 * silu_slope(z_two)).astype(jnp.bfloat16)
    weights_two = weight_grad(pooled_one, grad_two_field)
    back_one = conv_same(grad_two_field, flipped(kernel_two))
    grad_one_field = (spread_up(back_one) * 0.125 * silu_slope(z_one)).astype(jnp.bfloat16)
    weights_one = weight_grad(density, grad_one_field)
    grad_input = conv_same(grad_one_field, flipped(kernel_one)).astype(jnp.bfloat16)
    return (grad_input, unit_scale(weights_one), unit_scale(weights_two), unit_scale(weights_three))
```

```python
import functools

import jax
import jax.numpy as jnp
from jax import lax
from jax.experimental import pallas as pl
from jax.experimental.pallas import tpu as pltpu
from jax.sharding import PartitionSpec as P

MESH = pl.DeviceIdType.MESH

LOSS_SCALE = 1048576


conv_layout = ("NCDHW", "OIDHW", "NCDHW")


def with_halo(block, sides, width):
    for axis, dim in sides:
        count = lax.axis_size(axis)
        forward = [(i, i + 1) for i in range(count - 1)]
        backward = [(target, source) for source, target in forward]
        low = lax.ppermute(
            lax.slice_in_dim(block, block.shape[dim] - width, None, axis=dim), axis, forward
        )
        high = lax.ppermute(lax.slice_in_dim(block, 0, width, axis=dim), axis, backward)
        block = jnp.concatenate([low, block, high], axis=dim)
    return block


def conv_valid(haloed, kernel):
    result = lax.conv_general_dilated(
        haloed[None],
        kernel,
        (1, 1, 1),
        ((1, 1), (0, 0), (0, 0)),
        dimension_numbers=conv_layout,
        preferred_element_type=jnp.float32,
    )
    return result[0]


def flipped(kernel):
    return jnp.transpose(kernel, (1, 0, 2, 3, 4))[:, :, ::-1, ::-1, ::-1]


def silu_slope(values):
    sigmoid = jax.nn.sigmoid(values)
    return sigmoid * (1.0 + values * (1.0 - sigmoid))


def pooled(values):
    channels, depth_cells, row_cells, column_cells = values.shape
    return values.reshape(
        channels, depth_cells // 2, 2, row_cells // 2, 2, column_cells // 2, 2
    ).mean(axis=(2, 4, 6))


def spread_up(values):
    channels, depth_cells, row_cells, column_cells = values.shape
    grown = jnp.broadcast_to(
        values[:, :, None, :, None, :, None],
        (channels, depth_cells, 2, row_cells, 2, column_cells, 2),
    )
    return grown.reshape(channels, 2 * depth_cells, 2 * row_cells, 2 * column_cells)


def weight_term(haloed, gradient):
    outputs, depth_cells, row_cells, column_cells = gradient.shape
    padded = jnp.pad(haloed, ((0, 0), (1, 1), (0, 0), (0, 0)))
    shifted = [
        padded[
            :,
            depth_at : depth_at + depth_cells,
            row_at : row_at + row_cells,
            column_at : column_at + column_cells,
        ]
        for depth_at in range(3)
        for row_at in range(3)
        for column_at in range(3)
    ]
    stacked = jnp.stack(shifted, 0)
    term = jnp.einsum("odhw,tidhw->toi", gradient, stacked, preferred_element_type=jnp.float32)
    return jnp.transpose(term.reshape(3, 3, 3, outputs, -1), (3, 4, 0, 1, 2))


def unit_scale(gradient):
    return gradient / jnp.sqrt(jnp.mean(gradient * gradient) + 1e-06)


def act_rims(field, width):
    return with_halo(field, (("ha", 2), ("wa", 3)), width)


def grad_rims(field, width):
    return with_halo(field, (("ha", 2), ("wa", 3)), width)


def sum_everywhere_kernel(nh, nw, mine_ref, out_ref, slots, send_sem, recv_sem):
    count = nh * nw
    me = lax.axis_index("ha") * nw + lax.axis_index("wa")
    barrier = pltpu.get_barrier_semaphore()

    def greet(step, carry):
        peer = lax.rem(me + step, count)
        pl.semaphore_signal(
            barrier, inc=1, device_id=(peer // nw, lax.rem(peer, nw)), device_id_type=MESH
        )
        return carry

    lax.fori_loop(1, count, greet, 0)
    pl.semaphore_wait(barrier, count - 1)

    def copy_to(step):
        peer = lax.rem(me + step, count)
        return pltpu.make_async_remote_copy(
            src_ref=mine_ref,
            dst_ref=slots.at[step],
            send_sem=send_sem.at[step],
            recv_sem=recv_sem.at[step],
            device_id=(peer // nw, lax.rem(peer, nw)),
            device_id_type=MESH,
        )

    def begin(step, carry):
        copy_to(step).start()
        return carry

    def finish(step, carry):
        copy_to(step).wait()
        return carry

    lax.fori_loop(1, count, begin, 0)
    slots[0] = mine_ref[...]
    lax.fori_loop(1, count, finish, 0)
    out_ref[...] = jnp.sum(slots[...], axis=0)


def sum_everywhere(row):
    nh, nw = lax.axis_size("ha"), lax.axis_size("wa")
    return pl.pallas_call(
        functools.partial(sum_everywhere_kernel, nh, nw),
        out_shape=jax.ShapeDtypeStruct(row.shape, jnp.float32),
        in_specs=[pl.BlockSpec(memory_space=pltpu.VMEM)],
        out_specs=pl.BlockSpec(memory_space=pltpu.VMEM),
        scratch_shapes=[
            pltpu.VMEM((nh * nw,) + row.shape, jnp.float32),
            pltpu.SemaphoreType.DMA((nh * nw,)),
            pltpu.SemaphoreType.DMA((nh * nw,)),
        ],
        compiler_params=pltpu.CompilerParams(collective_id=0, has_side_effects=True),
    )(row)


def total_kernel(
    near, nw, far, src_ref, out_ref, got, part, got_far, own, all_far, *sems
):
    send_a, recv_a, send_b, recv_b, send_c, recv_c, send_d, recv_d = sems
    inner = near * nw
    row = lax.axis_index("ha")
    high, low = row // near, lax.rem(row, near)
    me = low * nw + lax.axis_index("wa")

    def inner_peer(step):
        at = lax.rem(me + step, inner)
        return at, (high * near + at // nw, lax.rem(at, nw))

    def far_peer(step):
        at = lax.rem(high + step, far)
        return at, (at * near + low, lax.axis_index("wa"))

    barrier = pltpu.get_barrier_semaphore()
    for step in range(1, inner):
        pl.semaphore_signal(
            barrier, inc=1, device_id=inner_peer(step)[1], device_id_type=MESH
        )
    for step in range(1, far):
        pl.semaphore_signal(barrier, inc=1, device_id=far_peer(step)[1], device_id_type=MESH)
    pl.semaphore_wait(barrier, inner + far - 2)

    def send(src, dst, sems, slot, where):
        copy = pltpu.make_async_remote_copy(
            src_ref=src,
            dst_ref=dst,
            send_sem=sems[0].at[slot],
            recv_sem=sems[1].at[slot],
            device_id=where,
            device_id_type=MESH,
        )
        copy.start()
        return copy

    copies = []
    for step in range(1, inner):
        at, where = inner_peer(step)
        copies.append(send(src_ref.at[at], got.at[step - 1], (send_a, recv_a), step - 1, where))
    total = src_ref[me].astype(jnp.float32)
    for step in range(1, inner):
        copies[step - 1].wait()
        total = total + got[step - 1].astype(jnp.float32)
    part[...] = total.astype(part.dtype)
    copies = []
    for step in range(1, far):
        at, where = far_peer(step)
        copies.append(send(part.at[at], got_far.at[step - 1], (send_b, recv_b), step - 1, where))
    total = part[high].astype(jnp.float32)
    for step in range(1, far):
        copies[step - 1].wait()
        total = total + got_far[step - 1].astype(jnp.float32)
    own[...] = total.astype(own.dtype)
    copies = []
    for step in range(1, far):
        at, where = far_peer(step)
        copies.append(send(own, all_far.at[high], (send_c, recv_c), step - 1, where))
    all_far[high] = own[...]
    for copy in copies:
        copy.wait()
    copies = []
    for step in range(1, inner):
        at, where = inner_peer(step)
        copies.append(send(all_far, out_ref.at[me], (send_d, recv_d), step - 1, where))
    out_ref[me] = all_far[...]
    for copy in copies:
        copy.wait()


def total_everywhere(terms):
    nh, nw = lax.axis_size("ha"), lax.axis_size("wa")
    near = 4 if nh % 4 == 0 else 1
    inner, far = near * nw, nh // near
    flat = jnp.concatenate([term.reshape(-1).astype(jnp.bfloat16) for term in terms])
    size = flat.shape[0]
    rows = -(-size // (128 * 16 * inner * far)) * 16
    flat = jnp.pad(flat, (0, inner * far * rows * 128 - size))
    src = flat.reshape(inner, far, rows, 128)
    dtype = jnp.bfloat16
    semaphores = []
    for slots in (inner, inner, far, far, far, far, inner, inner):
        semaphores.append(pltpu.SemaphoreType.DMA((slots,)))
    out = pl.pallas_call(
        functools.partial(total_kernel, near, nw, far),
        out_shape=jax.ShapeDtypeStruct(src.shape, dtype),
        in_specs=[pl.BlockSpec(memory_space=pltpu.VMEM)],
        out_specs=pl.BlockSpec(memory_space=pltpu.VMEM),
        scratch_shapes=[
            pltpu.VMEM((inner - 1, far, rows, 128), dtype),
            pltpu.VMEM((far, rows, 128), dtype),
            pltpu.VMEM((max(far - 1, 1), rows, 128), dtype),
            pltpu.VMEM((rows, 128), dtype),
            pltpu.VMEM((far, rows, 128), dtype),
        ]
        + semaphores,
        compiler_params=pltpu.CompilerParams(
            collective_id=1, has_side_effects=True, vmem_limit_bytes=32 * 1024 * 1024
        ),
    )(src)
    out = out.reshape(-1)
    results = []
    start = 0
    for term in terms:
        count = term.size
        results.append(out[start : start + count].astype(jnp.float32).reshape(term.shape))
        start += count
    return results


def narrow_conv(wide, kernel):
    outputs = kernel.shape[0]
    channels, depth_cells, row_cells, column_cells = wide.shape
    row_cells, column_cells = row_cells - 2, column_cells - 2
    taps = jnp.transpose(kernel, (2, 3, 4, 0, 1)).reshape(27 * outputs, channels)
    products = jnp.einsum("ki,idhw->kdhw", taps, wide, preferred_element_type=jnp.float32)
    products = products.reshape((3, 3, 3, outputs) + wide.shape[1:])
    products = jnp.pad(products, ((0, 0),) * 4 + ((1, 1), (0, 0), (0, 0)))
    total = 0.0
    for depth_at in range(3):
        for row_at in range(3):
            for column_at in range(3):
                total = total + products[
                    depth_at,
                    row_at,
                    column_at,
                    :,
                    depth_at : depth_at + depth_cells,
                    row_at : row_at + row_cells,
                    column_at : column_at + column_cells,
                ]
    return total


def local(
    density,
    kernel_one,
    kernel_two,
    kernel_three,
    dense_one,
    bias_one,
    dense_two,
    bias_two,
    dense_three,
    bias_three,
    target,
):
    row_cells = density.shape[2]
    column_cells = density.shape[3]
    input_wide = act_rims(density, 2)
    z_one_wide = conv_valid(input_wide, kernel_one)
    z_one = z_one_wide[:, :, 1:-1, 1:-1]
    near_input = input_wide[:, :, 1:-1, 1:-1]
    pooled_one = pooled(jax.nn.silu(z_one)).astype(jnp.bfloat16)
    near_one = act_rims(pooled_one, 1)
    z_two = conv_valid(near_one, kernel_two)
    pooled_two = pooled(jax.nn.silu(z_two)).astype(jnp.bfloat16)
    near_two = act_rims(pooled_two, 1)
    z_three = conv_valid(near_two, kernel_three)
    channels_three = z_three.shape[0]
    region_mean = jnp.mean(jax.nn.silu(z_three), axis=(1, 2, 3)).astype(jnp.bfloat16)
    place = (lax.axis_index("ha") * lax.axis_size("wa") + lax.axis_index("wa")) * channels_three
    own_rows = lax.dynamic_slice_in_dim(dense_one, place, channels_three, 0)
    own_part = jnp.dot(region_mean[None], own_rows, preferred_element_type=jnp.float32)
    pre_one = sum_everywhere(own_part)[0] + bias_one
    hidden_one = jax.nn.silu(pre_one)
    pre_two = (
        jnp.dot(hidden_one, dense_two.astype(jnp.float32), precision=lax.Precision.HIGHEST)
        + bias_two
    )
    hidden_two = jax.nn.silu(pre_two)
    output = (
        jnp.dot(hidden_two, dense_three.astype(jnp.float32), precision=lax.Precision.HIGHEST)
        + bias_three
    )
    grad_output = LOSS_SCALE * (output - target)
    grad_two = jnp.dot(
        dense_three.astype(jnp.float32), grad_output, precision=lax.Precision.HIGHEST
    ) * silu_slope(pre_two)
    grad_one = jnp.dot(
        dense_two.astype(jnp.float32), grad_two, precision=lax.Precision.HIGHEST
    ) * silu_slope(pre_one)
    grad_region = jnp.dot(own_rows.astype(jnp.float32), grad_one, precision=lax.Precision.HIGHEST)
    region_cells = z_three.shape[1] * z_three.shape[2] * z_three.shape[3]
    grad_three = (grad_region[:, None, None, None] / region_cells * silu_slope(z_three)).astype(
        jnp.bfloat16
    )
    wide_three = grad_rims(grad_three, 1)
    term_three = weight_term(near_two, grad_three)
    back_two = conv_valid(wide_three, flipped(kernel_three))
    grad_two_field = (spread_up(back_two) * 0.125 * silu_slope(z_two)).astype(jnp.bfloat16)
    term_two = weight_term(near_one, grad_two_field)
    wide_two = grad_rims(grad_two_field, 2)
    back_one = conv_valid(wide_two, flipped(kernel_two))
    margin_back = spread_up(back_one)[:, :, 1:-1, 1:-1]
    rows_global = lax.axis_index("ha") * row_cells + jnp.arange(-1, row_cells + 1, dtype=jnp.int32)
    columns_global = lax.axis_index("wa") * column_cells + jnp.arange(
        -1, column_cells + 1, dtype=jnp.int32
    )
    inside_rows = (rows_global >= 0) & (rows_global < row_cells * lax.axis_size("ha"))
    inside_columns = (columns_global >= 0) & (columns_global < column_cells * lax.axis_size("wa"))
    inside = (inside_rows[:, None] & inside_columns[None, :]).astype(jnp.float32)
    grad_one_wide = (margin_back * 0.125 * silu_slope(z_one_wide) * inside).astype(jnp.bfloat16)
    grad_one_field = grad_one_wide[:, :, 1:-1, 1:-1]
    term_one = weight_term(near_input, grad_one_field)
    grad_input = narrow_conv(grad_one_wide, flipped(kernel_one)).astype(jnp.bfloat16)
    weights_one, weights_two, weights_three = total_everywhere((term_one, term_two, term_three))
    return (grad_input, unit_scale(weights_one), unit_scale(weights_two), unit_scale(weights_three))


def solution(mesh):
    in_specs = (P(None, None, "ha", "wa"), P(), P(), P(), P(), P(), P(), P(), P(), P(), P())
    out_specs = (P(None, None, "ha", "wa"), P(), P(), P())
    return jax.shard_map(local, mesh=mesh, in_specs=in_specs, out_specs=out_specs, check_vma=False)
```

```python
import functools

import jax
import jax.numpy as jnp
from jax import lax
from jax.experimental import pallas as pl
from jax.experimental.pallas import tpu as pltpu
from jax.sharding import PartitionSpec as P

MESH = pl.DeviceIdType.MESH

LOSS_SCALE = 1048576


conv_layout = ("NCDHW", "OIDHW", "NCDHW")


def with_halo(block, sides, width):
    for axis, dim in sides:
        count = lax.axis_size(axis)
        forward = [(i, i + 1) for i in range(count - 1)]
        backward = [(target, source) for source, target in forward]
        low = lax.ppermute(
            lax.slice_in_dim(block, block.shape[dim] - width, None, axis=dim), axis, forward
        )
        high = lax.ppermute(lax.slice_in_dim(block, 0, width, axis=dim), axis, backward)
        block = jnp.concatenate([low, block, high], axis=dim)
    return block


def conv_valid(haloed, kernel):
    result = lax.conv_general_dilated(
        haloed[None],
        kernel,
        (1, 1, 1),
        ((1, 1), (0, 0), (0, 0)),
        dimension_numbers=conv_layout,
        preferred_element_type=jnp.float32,
    )
    return result[0]


def flipped(kernel):
    return jnp.transpose(kernel, (1, 0, 2, 3, 4))[:, :, ::-1, ::-1, ::-1]


def silu_slope(values):
    sigmoid = jax.nn.sigmoid(values)
    return sigmoid * (1.0 + values * (1.0 - sigmoid))


def pooled(values):
    channels, depth_cells, row_cells, column_cells = values.shape
    return values.reshape(
        channels, depth_cells // 2, 2, row_cells // 2, 2, column_cells // 2, 2
    ).mean(axis=(2, 4, 6))


def spread_up(values):
    channels, depth_cells, row_cells, column_cells = values.shape
    grown = jnp.broadcast_to(
        values[:, :, None, :, None, :, None],
        (channels, depth_cells, 2, row_cells, 2, column_cells, 2),
    )
    return grown.reshape(channels, 2 * depth_cells, 2 * row_cells, 2 * column_cells)


def weight_term(haloed, gradient):
    outputs, depth_cells, row_cells, column_cells = gradient.shape
    padded = jnp.pad(haloed, ((0, 0), (1, 1), (0, 0), (0, 0)))
    shifted = [
        padded[
            :,
            depth_at : depth_at + depth_cells,
            row_at : row_at + row_cells,
            column_at : column_at + column_cells,
        ]
        for depth_at in range(3)
        for row_at in range(3)
        for column_at in range(3)
    ]
    stacked = jnp.stack(shifted, 0)
    term = jnp.einsum("odhw,tidhw->toi", gradient, stacked, preferred_element_type=jnp.float32)
    return jnp.transpose(term.reshape(3, 3, 3, outputs, -1), (3, 4, 0, 1, 2))


def unit_scale(gradient):
    return gradient / jnp.sqrt(jnp.mean(gradient * gradient) + 1e-06)


def act_rims(field, width):
    return with_halo(field, (("ha", 2), ("wa", 3)), width)


def grad_rims(field, width):
    return with_halo(field, (("ha", 2), ("wa", 3)), width)


def sum_everywhere_kernel(nh, nw, mine_ref, out_ref, slots, send_sem, recv_sem):
    count = nh * nw
    me = lax.axis_index("ha") * nw + lax.axis_index("wa")
    barrier = pltpu.get_barrier_semaphore()

    def greet(step, carry):
        peer = lax.rem(me + step, count)
        pl.semaphore_signal(
            barrier, inc=1, device_id=(peer // nw, lax.rem(peer, nw)), device_id_type=MESH
        )
        return carry

    lax.fori_loop(1, count, greet, 0)
    pl.semaphore_wait(barrier, count - 1)

    def copy_to(step):
        peer = lax.rem(me + step, count)
        return pltpu.make_async_remote_copy(
            src_ref=mine_ref,
            dst_ref=slots.at[step],
            send_sem=send_sem.at[step],
            recv_sem=recv_sem.at[step],
            device_id=(peer // nw, lax.rem(peer, nw)),
            device_id_type=MESH,
        )

    def begin(step, carry):
        copy_to(step).start()
        return carry

    def finish(step, carry):
        copy_to(step).wait()
        return carry

    lax.fori_loop(1, count, begin, 0)
    slots[0] = mine_ref[...]
    lax.fori_loop(1, count, finish, 0)
    out_ref[...] = jnp.sum(slots[...], axis=0)


def sum_everywhere(row):
    nh, nw = lax.axis_size("ha"), lax.axis_size("wa")
    return pl.pallas_call(
        functools.partial(sum_everywhere_kernel, nh, nw),
        out_shape=jax.ShapeDtypeStruct(row.shape, jnp.float32),
        in_specs=[pl.BlockSpec(memory_space=pltpu.VMEM)],
        out_specs=pl.BlockSpec(memory_space=pltpu.VMEM),
        scratch_shapes=[
            pltpu.VMEM((nh * nw,) + row.shape, jnp.float32),
            pltpu.SemaphoreType.DMA((nh * nw,)),
            pltpu.SemaphoreType.DMA((nh * nw,)),
        ],
        compiler_params=pltpu.CompilerParams(collective_id=0, has_side_effects=True),
    )(row)


def narrow_conv(wide, kernel):
    outputs = kernel.shape[0]
    channels, depth_cells, row_cells, column_cells = wide.shape
    row_cells, column_cells = row_cells - 2, column_cells - 2
    taps = jnp.transpose(kernel, (2, 3, 4, 0, 1)).reshape(27 * outputs, channels)
    products = jnp.einsum("ki,idhw->kdhw", taps, wide, preferred_element_type=jnp.float32)
    products = products.reshape((3, 3, 3, outputs) + wide.shape[1:])
    products = jnp.pad(products, ((0, 0),) * 4 + ((1, 1), (0, 0), (0, 0)))
    total = 0.0
    for depth_at in range(3):
        for row_at in range(3):
            for column_at in range(3):
                total = total + products[
                    depth_at,
                    row_at,
                    column_at,
                    :,
                    depth_at : depth_at + depth_cells,
                    row_at : row_at + row_cells,
                    column_at : column_at + column_cells,
                ]
    return total


def local(
    density,
    kernel_one,
    kernel_two,
    kernel_three,
    dense_one,
    bias_one,
    dense_two,
    bias_two,
    dense_three,
    bias_three,
    target,
):
    row_cells = density.shape[2]
    column_cells = density.shape[3]
    input_wide = act_rims(density, 2)
    z_one_wide = conv_valid(input_wide, kernel_one)
    z_one = z_one_wide[:, :, 1:-1, 1:-1]
    near_input = input_wide[:, :, 1:-1, 1:-1]
    pooled_one = pooled(jax.nn.silu(z_one)).astype(jnp.bfloat16)
    near_one = act_rims(pooled_one, 1)
    z_two = conv_valid(near_one, kernel_two)
    pooled_two = pooled(jax.nn.silu(z_two)).astype(jnp.bfloat16)
    near_two = act_rims(pooled_two, 1)
    z_three = conv_valid(near_two, kernel_three)
    channels_three = z_three.shape[0]
    region_mean = jnp.mean(jax.nn.silu(z_three), axis=(1, 2, 3)).astype(jnp.bfloat16)
    place = (lax.axis_index("ha") * lax.axis_size("wa") + lax.axis_index("wa")) * channels_three
    own_rows = lax.dynamic_slice_in_dim(dense_one, place, channels_three, 0)
    own_part = jnp.dot(region_mean[None], own_rows, preferred_element_type=jnp.float32)
    pre_one = sum_everywhere(own_part)[0] + bias_one
    hidden_one = jax.nn.silu(pre_one)
    pre_two = (
        jnp.dot(hidden_one, dense_two.astype(jnp.float32), precision=lax.Precision.HIGHEST)
        + bias_two
    )
    hidden_two = jax.nn.silu(pre_two)
    output = (
        jnp.dot(hidden_two, dense_three.astype(jnp.float32), precision=lax.Precision.HIGHEST)
        + bias_three
    )
    grad_output = LOSS_SCALE * (output - target)
    grad_two = jnp.dot(
        dense_three.astype(jnp.float32), grad_output, precision=lax.Precision.HIGHEST
    ) * silu_slope(pre_two)
    grad_one = jnp.dot(
        dense_two.astype(jnp.float32), grad_two, precision=lax.Precision.HIGHEST
    ) * silu_slope(pre_one)
    grad_region = jnp.dot(own_rows.astype(jnp.float32), grad_one, precision=lax.Precision.HIGHEST)
    region_cells = z_three.shape[1] * z_three.shape[2] * z_three.shape[3]
    grad_three = (grad_region[:, None, None, None] / region_cells * silu_slope(z_three)).astype(
        jnp.bfloat16
    )
    wide_three = grad_rims(grad_three, 1)
    term_three = weight_term(near_two, grad_three)
    back_two = conv_valid(wide_three, flipped(kernel_three))
    grad_two_field = (spread_up(back_two) * 0.125 * silu_slope(z_two)).astype(jnp.bfloat16)
    term_two = weight_term(near_one, grad_two_field)
    wide_two = grad_rims(grad_two_field, 2)
    back_one = conv_valid(wide_two, flipped(kernel_two))
    margin_back = spread_up(back_one)[:, :, 1:-1, 1:-1]
    rows_global = lax.axis_index("ha") * row_cells + jnp.arange(-1, row_cells + 1, dtype=jnp.int32)
    columns_global = lax.axis_index("wa") * column_cells + jnp.arange(
        -1, column_cells + 1, dtype=jnp.int32
    )
    inside_rows = (rows_global >= 0) & (rows_global < row_cells * lax.axis_size("ha"))
    inside_columns = (columns_global >= 0) & (columns_global < column_cells * lax.axis_size("wa"))
    inside = (inside_rows[:, None] & inside_columns[None, :]).astype(jnp.float32)
    grad_one_wide = (margin_back * 0.125 * silu_slope(z_one_wide) * inside).astype(jnp.bfloat16)
    grad_one_field = grad_one_wide[:, :, 1:-1, 1:-1]
    term_one = weight_term(near_input, grad_one_field)
    grad_input = narrow_conv(grad_one_wide, flipped(kernel_one)).astype(jnp.bfloat16)
    weights_one, weights_two, weights_three = lax.psum(
        (term_one, term_two, term_three), ("ha", "wa")
    )
    return (grad_input, unit_scale(weights_one), unit_scale(weights_two), unit_scale(weights_three))


def solution(mesh):
    in_specs = (P(None, None, "ha", "wa"), P(), P(), P(), P(), P(), P(), P(), P(), P(), P())
    out_specs = (P(None, None, "ha", "wa"), P(), P(), P())
    return jax.shard_map(local, mesh=mesh, in_specs=in_specs, out_specs=out_specs, check_vma=False)
```
